1024 devices in a mesh: tensor: 8 (over z_hi, core), replica: 16 (over x, z_lo), fsdp: 8 (over y).
Axes of the slice: x: 8, y: 8, z: 8 (z_hi: 4, z_lo: 2; z = z_hi * 2 + z_lo), core: 2. Of those that a mesh axis runs over, the one named last changes fastest.
Arguments:
- gradients: bfloat16 [16, 2048, 28672], P('replica', 'fsdp', 'tensor'), may hold values from -6 to 6
- seeds: int32 [2], replicated, may hold values from 0 to 1073741823
- adam_step: int32 [1], replicated, may hold values from 1 to 8
- first_moment: float32 [2048, 28672], P(('fsdp', 'replica'), 'tensor'), may hold values from -0.6 to 0.6
- second_moment: float32 [2048, 28672], P(('fsdp', 'replica'), 'tensor'), may hold values from 0.001 to 0.1
Outputs:
- new_first: float32 [2048, 28672], P(('fsdp', 'replica'), 'tensor')
- new_second: float32 [2048, 28672], P(('fsdp', 'replica'), 'tensor')
- step_update: float32 [2048, 28672], P(('fsdp', 'replica'), 'tensor')
The draws below stay inside these ranges and needn't reach their ends.
All inputs are finite; a program needn't handle non-finite values.
Results may differ from the reference program's by a relative error of at most 0.012.
The reference program's roundings to bfloat16 on the way (of `projection` and `sketch_rounded`) count: a program that leaves them out, or rounds other values in their place, can miss the bound.
Values may be sent and summed in bfloat16 or wider, within the bound.
A program may use at most 32 MiB of HBM per device.

```python
import math
import jax
import jax.numpy as jnp
from jax import lax

FF = 28672
RANK = 512
ROWS = 2048
N_REPLICA = 16


def block_scale(own_key, shape, pieces, smallest, top_value):
    def one(dim, shards_of):
        steps = jax.random.uniform(jax.random.fold_in(jax.random.fold_in(own_key, 6), dim), (shards_of,), jnp.float32, smallest / len(pieces), top_value / len(pieces))
        return jnp.repeat(jnp.exp(steps), shape[dim] // shards_of).reshape((-1,) + (1,) * (len(shape) - dim - 1))

    factor_of = one(*pieces[0])
    for cut in pieces[1:]:
        factor_of = factor_of * one(*cut)
    return factor_of


def normal_values(stream_key, dims, scale, bound, split=(), held_as=jnp.bfloat16):
    values = jax.random.normal(stream_key, dims, jnp.float32) * scale
    if len(split) > 0:
        values = block_scale(stream_key, dims, split, -0.22, 0.18) * values
    return jnp.clip(values, min=-bound, max=bound).astype(held_as)


def setup_inputs(seed: int = 0) -> dict:
    streams_of = jax.random.split(jax.random.key(seed), 6)
    return {
        "gradients": normal_values(streams_of[0], (N_REPLICA, ROWS, FF), 1.0, 6.0, ((0, 16), (1, 8), (2, 8))),
        "seeds": jax.random.randint(streams_of[1], (2,), 0, 1073741824).astype(jnp.int32),
        "adam_step": jax.random.randint(streams_of[2], (1,), 1, 9).astype(jnp.int32),
        "first_moment": normal_values(streams_of[3], (ROWS, FF), 0.1, 0.6, ((0, 128), (1, 8)), jnp.float32),
        "second_moment": jnp.clip(jnp.exp(math.log(0.1) - 4.6051702 * jax.random.uniform(streams_of[4], (ROWS, FF), jnp.float32) ** block_scale(streams_of[4], (ROWS, FF), ((0, 128), (1, 8)), -0.2, 0.2)), 0.001, 0.1),
    }


def scramble(value):
    value = value ^ lax.shift_right_logical(value, jnp.full_like(value, 16))
    value = value * jnp.int32(-2048144789)
    value = value ^ lax.shift_right_logical(value, jnp.full_like(value, 13))
    value = value * jnp.int32(-1028477387)
    value = value ^ lax.shift_right_logical(value, jnp.full_like(value, 16))
    return value

def projection_block(first_column, columns, rank, seeds):
    seed_key = seeds[0] ^ seeds[1] * jnp.int32(668265263)
    column = lax.broadcasted_iota(jnp.int32, (columns, rank), 0) + first_column
    entry = lax.broadcasted_iota(jnp.int32, (columns, rank), 1)
    counter = (column * jnp.int32(rank) + entry) * jnp.int32(2)
    hash_a = scramble(counter * jnp.int32(-1640531535) ^ seed_key)
    hash_b = scramble((counter + jnp.int32(1)) * jnp.int32(-1640531535) ^ seed_key)
    inverse = 1.0 / 16777216.0
    uniform_a = (lax.shift_right_logical(hash_a, jnp.full_like(hash_a, 8)).astype(jnp.float32) + 0.5) * inverse
    uniform_b = (lax.shift_right_logical(hash_b, jnp.full_like(hash_b, 8)).astype(jnp.float32) + 0.5) * inverse
    gauss = jnp.sqrt(-2.0 * jnp.log(uniform_a)) * jnp.cos(6.283185307179586 * uniform_b)
    return (gauss * rank ** (-0.5)).astype(jnp.bfloat16)

def reference(gradients, seeds, adam_step, first_moment, second_moment):
    projection = projection_block(jnp.int32(0), FF, RANK, seeds)
    wide_proj = projection.astype(jnp.float32)

    def accumulate(total, block):
        return (total + block.astype(jnp.float32), None)
    total, _ = lax.scan(accumulate, jnp.zeros((ROWS, FF), jnp.float32), gradients)
    sketch = jnp.dot(total, wide_proj, precision=lax.Precision.HIGHEST) * (1.0 / N_REPLICA)
    sketch_rounded = sketch.astype(jnp.bfloat16)
    estimate = jnp.dot(sketch_rounded.astype(jnp.float32), wide_proj.T, precision=lax.Precision.HIGHEST)
    new_first = 0.9 * first_moment + 0.1 * estimate
    new_second = 0.95 * second_moment + 0.05 * estimate * estimate
    step_float = adam_step[0].astype(jnp.float32)
    fix_first = 1.0 - jnp.power(jnp.float32(0.9), step_float)
    fix_second = 1.0 - jnp.power(jnp.float32(0.95), step_float)
    step_update = new_first / fix_first / (jnp.sqrt(new_second / fix_second) + 1e-08)
    return (new_first, new_second, step_update)
```

```python
import jax
import jax.numpy as jnp
from jax import lax
from jax.experimental import pallas as pl
from jax.experimental.pallas import tpu as pltpu
from jax.sharding import PartitionSpec as P

RANK = 512
COLUMNS = 3584
WIDTH = 128
DEPTH = 512
CHUNKS = RANK // WIDTH
BLOCKS = COLUMNS // DEPTH
STEPS = CHUNKS * BLOCKS
WEYL = -1640531535
MESH = pl.DeviceIdType.MESH
SINE = (6.28317941 / 16, -41.33894249 / 16, 81.39535834 / 16, -71.47469135 / 16)


def srl(value, bits):
    return lax.shift_right_logical(value, jnp.full_like(value, bits))


def scramble(value):
    value = value ^ srl(value, 16)
    value = value * jnp.int32(-2048144789)
    value = value ^ srl(value, 13)
    value = value * jnp.int32(-1028477387)
    return value ^ srl(value, 16)


def entries(counted, seed_key):
    hash_a = scramble(counted ^ seed_key)
    hash_b = scramble((counted + jnp.int32(WEYL)) ^ seed_key)
    negative_log = 16.635532333438686 - jnp.log(srl(hash_a, 8).astype(jnp.float32) + 0.5)
    radius = negative_log * lax.rsqrt(jnp.maximum(negative_log, 1e-30))
    turn = lax.shift_right_arithmetic(hash_b, jnp.full_like(hash_b, 8)).astype(jnp.float32) + 0.5
    z = 0.25 - jnp.abs(turn) * (1.0 / 16777216.0)
    square = z * z
    poly = SINE[3] * square + SINE[2]
    poly = poly * square + SINE[1]
    poly = poly * square + SINE[0]
    return (poly * z) * radius


def kernel(
    gradient_ref, seeds_ref, out_ref,
    grad, proj, base, acc, got1, out2, got2, out3, got3, sketch,
    grad_sem, send1, recv1, send2, recv2, send3, recv3,
):
    tensor = lax.axis_index("tensor")
    replica = lax.axis_index("replica")
    core = lax.rem(tensor, 2)
    z_hi = lax.div(tensor, 2)
    x = lax.div(replica, 2)
    z_lo = lax.rem(replica, 2)
    same = core == z_lo
    z = z_hi * 2 + z_lo

    def x_peer(step):
        return lax.rem(x + step, 8)

    barrier = pltpu.get_barrier_semaphore()
    pl.semaphore_signal(
        barrier, inc=1, device_id={"tensor": z_hi * 2 + 1 - core}, device_id_type=MESH
    )
    for step in range(1, 8):
        pl.semaphore_signal(
            barrier, inc=1, device_id={"replica": x_peer(step) * 2 + z_lo}, device_id_type=MESH
        )
    for far in range(8):
        far_hi, far_lo = far // 2, far % 2

        @pl.when(jnp.logical_or(far != z, jnp.logical_not(same)))
        def _():
            pl.semaphore_signal(
                barrier,
                inc=1,
                device_id={"tensor": far_hi * 2 + z_lo, "replica": x * 2 + far_lo},
                device_id_type=MESH,
            )

    def grad_copy(block):
        return pltpu.make_async_copy(
            gradient_ref.at[:, pl.ds(block * DEPTH, DEPTH)], grad.at[block], grad_sem.at[block]
        )

    for block in range(BLOCKS):
        grad_copy(block).start()

    seed_key = seeds_ref[0] ^ (seeds_ref[1] * jnp.int32(668265263))
    rows = lax.broadcasted_iota(jnp.int32, (DEPTH, WIDTH), 0)
    lanes = lax.broadcasted_iota(jnp.int32, (DEPTH, WIDTH), 1)
    base[...] = (rows * jnp.int32(RANK) + lanes) * jnp.int32(2) * jnp.int32(WEYL)
    first_column = tensor * COLUMNS

    def generate(index):
        chunk = lax.div(index, BLOCKS)
        block = lax.rem(index, BLOCKS)
        column = first_column + block * DEPTH
        offset = (column * jnp.int32(RANK) + chunk * WIDTH) * jnp.int32(2) * jnp.int32(WEYL)
        proj[index] = entries(base[...] + offset, seed_key).astype(jnp.bfloat16)

    def multiply(index):
        chunk = lax.div(index, BLOCKS)
        block = lax.rem(index, BLOCKS)
        part = jnp.dot(grad[block], proj[index], preferred_element_type=jnp.float32)
        part = part.reshape(8, 2, 16, WIDTH)
        acc[chunk] = jnp.where(block == 0, 0.0, acc[chunk]) + part

    def copy1(chunk):
        return pltpu.make_async_remote_copy(
            src_ref=acc.at[chunk, :, 1 - core],
            dst_ref=got1.at[chunk],
            send_sem=send1.at[chunk],
            recv_sem=recv1.at[chunk],
            device_id={"tensor": z_hi * 2 + 1 - core},
            device_id_type=MESH,
        )

    def copy2(chunk, step):
        return pltpu.make_async_remote_copy(
            src_ref=out2.at[chunk, x_peer(step)],
            dst_ref=got2.at[chunk, x],
            send_sem=send2.at[chunk, step],
            recv_sem=recv2.at[chunk, x],
            device_id={"replica": x_peer(step) * 2 + z_lo},
            device_id_type=MESH,
        )

    def arrive2(chunk, step):
        return pltpu.make_async_remote_copy(
            src_ref=out2.at[chunk, x],
            dst_ref=got2.at[chunk, x_peer(step)],
            send_sem=send2.at[chunk, step],
            recv_sem=recv2.at[chunk, x_peer(step)],
            device_id={"replica": x_peer(step) * 2 + z_lo},
            device_id_type=MESH,
        )

    def copy3(chunk, target):
        return pltpu.make_async_remote_copy(
            src_ref=out3.at[chunk],
            dst_ref=got3.at[chunk, z],
            send_sem=send3.at[chunk, target],
            recv_sem=recv3.at[chunk, z],
            device_id={"tensor": target, "replica": x * 2 + core},
            device_id_type=MESH,
        )

    def arrive3(chunk, far):
        return pltpu.make_async_remote_copy(
            src_ref=out3.at[chunk],
            dst_ref=got3.at[chunk, far],
            send_sem=send3.at[chunk, far],
            recv_sem=recv3.at[chunk, far],
            device_id={"tensor": (far // 2) * 2 + z_lo, "replica": x * 2 + far % 2},
            device_id_type=MESH,
        )

    def not_self(target):
        return jnp.logical_or(target != tensor, jnp.logical_not(same))

    def stage1(chunk):
        copy1(chunk).start()

    def stage2(chunk):
        copy1(chunk).wait_recv()
        total = acc[chunk, :, core] + got1[chunk]
        out2[chunk] = total.astype(jnp.bfloat16)
        for step in range(1, 8):
            copy2(chunk, step).start()

    def stage3(chunk):
        total = acc[chunk, x, core] + got1[chunk, x]
        for step in range(1, 8):
            arrive2(chunk, step).wait_recv()
            total = total + got2[chunk, x_peer(step)].astype(jnp.float32)
        out3[chunk] = total.astype(jnp.bfloat16)
        for target in range(8):

            @pl.when(not_self(target))
            def _():
                copy3(chunk, target).start()

        @pl.when(same)
        def _():
            got3[chunk, z] = out3[chunk]

    def finish(chunk):
        for far in range(8):

            @pl.when(jnp.logical_or(far != z, jnp.logical_not(same)))
            def _():
                arrive3(chunk, far).wait_recv()

        total = jnp.zeros((16, WIDTH), jnp.float32)
        for far in range(8):
            total = total + got3[chunk, far].astype(jnp.float32)
        sketch[chunk] = (total * (1.0 / 16)).astype(jnp.bfloat16)

    def back(chunk, index):
        return lax.dot_general(
            sketch[chunk],
            proj[chunk * BLOCKS + index],
            (((1,), (1,)), ((), ())),
            preferred_element_type=jnp.float32,
        )

    generate(0)
    for block in range(BLOCKS):
        grad_copy(block).wait()

    pl.semaphore_wait(barrier, jnp.where(same, 15, 16))

    def body(index, carry):
        multiply(index - 1)
        generate(index)
        chunk = lax.div(index, BLOCKS) - 1
        phase = lax.rem(index, BLOCKS)
        for at, work in ((0, stage1), (2, stage2), (4, stage3), (6, finish)):

            @pl.when(jnp.logical_and(chunk >= 0, phase == at))
            def _():
                work(chunk)

        return carry

    lax.fori_loop(1, STEPS, body, 0)
    last = CHUNKS - 1
    multiply(STEPS - 1)
    stage1(last)
    stage2(last)
    for block in range(BLOCKS):
        total = back(0, block)
        for chunk in range(1, last):
            total = total + back(chunk, block)
        out_ref[:, block * DEPTH : (block + 1) * DEPTH] = total
    stage3(last)
    finish(last)
    for block in range(BLOCKS):
        out_ref[:, block * DEPTH : (block + 1) * DEPTH] += back(last, block)
    for chunk in range(CHUNKS):
        copy1(chunk).wait_send()
        for step in range(1, 8):
            copy2(chunk, step).wait_send()
        for target in range(8):

            @pl.when(not_self(target))
            def _():
                copy3(chunk, target).wait_send()


def per_device(gradients, seeds, adam_step, first_moment, second_moment):
    gradient = gradients[0]
    dma = pltpu.SemaphoreType.DMA
    estimate = pl.pallas_call(
        kernel,
        out_shape=jax.ShapeDtypeStruct((16, COLUMNS), jnp.float32),
        in_specs=[
            pl.BlockSpec(memory_space=pl.ANY),
            pl.BlockSpec(memory_space=pltpu.SMEM),
        ],
        out_specs=pl.BlockSpec(memory_space=pltpu.VMEM),
        scratch_shapes=[
            pltpu.VMEM((BLOCKS, 256, DEPTH), jnp.bfloat16),
            pltpu.VMEM((STEPS, DEPTH, WIDTH), jnp.bfloat16),
            pltpu.VMEM((DEPTH, WIDTH), jnp.int32),
            pltpu.VMEM((CHUNKS, 8, 2, 16, WIDTH), jnp.float32),
            pltpu.VMEM((CHUNKS, 8, 16, WIDTH), jnp.float32),
            pltpu.VMEM((CHUNKS, 8, 16, WIDTH), jnp.bfloat16),
            pltpu.VMEM((CHUNKS, 8, 16, WIDTH), jnp.bfloat16),
            pltpu.VMEM((CHUNKS, 16, WIDTH), jnp.bfloat16),
            pltpu.VMEM((CHUNKS, 8, 16, WIDTH), jnp.bfloat16),
            pltpu.VMEM((CHUNKS, 16, WIDTH), jnp.bfloat16),
            dma((BLOCKS,)),
            dma((CHUNKS,)),
            dma((CHUNKS,)),
            dma((CHUNKS, 8)),
            dma((CHUNKS, 8)),
            dma((CHUNKS, 8)),
            dma((CHUNKS, 8)),
        ],
        compiler_params=pltpu.CompilerParams(
            collective_id=0, has_side_effects=True, vmem_limit_bytes=24 << 20
        ),
        cost_estimate=pl.CostEstimate(
            flops=2 * 256 * COLUMNS * RANK, bytes_accessed=3 << 20, transcendentals=0
        ),
    )(gradient, seeds)
    new_first = 0.9 * first_moment + 0.1 * estimate
    new_second = 0.95 * second_moment + 0.05 * estimate * estimate
    step_float = adam_step[0].astype(jnp.float32)
    fix_first = 1.0 - jnp.power(jnp.float32(0.9), step_float)
    fix_second = 1.0 - jnp.power(jnp.float32(0.95), step_float)
    step_update = new_first / fix_first / (jnp.sqrt(new_second / fix_second) + 1e-08)
    return (new_first, new_second, step_update)


def solution(mesh):
    rows = P(("fsdp", "replica"), "tensor")
    return jax.shard_map(
        per_device,
        mesh=mesh,
        in_specs=(P("replica", "fsdp", "tensor"), P(), P(), rows, rows),
        out_specs=(rows, rows, rows),
        check_vma=False,
    )
```

```python
import jax
import jax.numpy as jnp
from jax import lax
from jax.experimental import pallas as pl
from jax.experimental.pallas import tpu as pltpu
from jax.sharding import PartitionSpec as P

RANK = 512
COLUMNS = 3584
WIDTH = 256
DEPTH = 256
PIECE = 896
PIECES = COLUMNS // PIECE
CHUNKS = RANK // WIDTH
BLOCKS = COLUMNS // DEPTH
WEYL = -1640531535
MESH = pl.DeviceIdType.MESH
SINE = (6.28317941 / 16, -41.33894249 / 16, 81.39535834 / 16, -71.47469135 / 16)


def srl(value, bits):
    return lax.shift_right_logical(value, jnp.full_like(value, bits))


def scramble(value):
    value = value ^ srl(value, 16)
    value = value * jnp.int32(-2048144789)
    value = value ^ srl(value, 13)
    value = value * jnp.int32(-1028477387)
    return value ^ srl(value, 16)


def entries(counted, seed_key):
    hash_a = scramble(counted ^ seed_key)
    hash_b = scramble((counted + jnp.int32(WEYL)) ^ seed_key)
    negative_log = 16.635532333438686 - jnp.log(srl(hash_a, 8).astype(jnp.float32) + 0.5)
    radius = negative_log * lax.rsqrt(jnp.maximum(negative_log, 1e-30))
    turn = lax.shift_right_arithmetic(hash_b, jnp.full_like(hash_b, 8)).astype(jnp.float32) + 0.5
    z = 0.25 - jnp.abs(turn) * (1.0 / 16777216.0)
    square = z * z
    poly = SINE[3] * square + SINE[2]
    poly = poly * square + SINE[1]
    poly = poly * square + SINE[0]
    return (poly * z) * radius


def kernel(
    gradient_ref, seeds_ref, out_ref,
    grad, proj, base, acc, got1, out2, got2, out3, got3, sketch,
    grad_sem, send1, recv1, send2, recv2, send3, recv3,
):
    tensor = lax.axis_index("tensor")
    replica = lax.axis_index("replica")
    core = lax.rem(tensor, 2)
    z_hi = lax.div(tensor, 2)
    x = lax.div(replica, 2)
    z_lo = lax.rem(replica, 2)
    same = core == z_lo
    z = z_hi * 2 + z_lo

    def x_peer(step):
        return lax.rem(x + step, 8)

    barrier = pltpu.get_barrier_semaphore()
    pl.semaphore_signal(
        barrier, inc=1, device_id={"tensor": z_hi * 2 + 1 - core}, device_id_type=MESH
    )
    for step in range(1, 8):
        pl.semaphore_signal(
            barrier, inc=1, device_id={"replica": x_peer(step) * 2 + z_lo}, device_id_type=MESH
        )
    for far in range(8):
        far_hi, far_lo = far // 2, far % 2

        @pl.when(jnp.logical_or(far != z, jnp.logical_not(same)))
        def _():
            pl.semaphore_signal(
                barrier,
                inc=1,
                device_id={"tensor": far_hi * 2 + z_lo, "replica": x * 2 + far_lo},
                device_id_type=MESH,
            )

    def grad_copy(piece):
        return pltpu.make_async_copy(
            gradient_ref.at[:, pl.ds(piece * PIECE, PIECE)], grad.at[piece], grad_sem.at[piece]
        )

    for piece in range(PIECES):
        grad_copy(piece).start()

    seed_key = seeds_ref[0] ^ (seeds_ref[1] * jnp.int32(668265263))
    rows = lax.broadcasted_iota(jnp.int32, (DEPTH, WIDTH), 0)
    lanes = lax.broadcasted_iota(jnp.int32, (DEPTH, WIDTH), 1)
    base[...] = (rows * jnp.int32(RANK) + lanes) * jnp.int32(2) * jnp.int32(WEYL)
    first_column = tensor * COLUMNS

    def generate(chunk, lower, upper):
        def step(block, carry):
            start = pl.multiple_of(block * DEPTH, DEPTH)
            column = first_column + start
            offset = (column * jnp.int32(RANK) + chunk * WIDTH) * jnp.int32(2) * jnp.int32(WEYL)
            made = entries(base[...] + offset, seed_key).astype(jnp.bfloat16)
            proj[chunk, pl.ds(start, DEPTH), :] = made
            return carry

        lax.fori_loop(lower, upper, step, 0)

    def multiply(chunk):
        part = None
        for piece in range(PIECES):
            term = jnp.dot(
                grad[piece],
                proj[chunk, piece * PIECE : (piece + 1) * PIECE, :],
                preferred_element_type=jnp.float32,
            )
            part = term if part is None else part + term
        acc[chunk] = part.reshape(8, 2, 16, WIDTH)

    def copy1(chunk):
        return pltpu.make_async_remote_copy(
            src_ref=acc.at[chunk, :, 1 - core],
            dst_ref=got1.at[chunk],
            send_sem=send1.at[chunk],
            recv_sem=recv1.at[chunk],
            device_id={"tensor": z_hi * 2 + 1 - core},
            device_id_type=MESH,
        )

    def copy2(chunk, step):
        return pltpu.make_async_remote_copy(
            src_ref=out2.at[chunk, x_peer(step)],
            dst_ref=got2.at[chunk, x],
            send_sem=send2.at[chunk, step],
            recv_sem=recv2.at[chunk, x],
            device_id={"replica": x_peer(step) * 2 + z_lo},
            device_id_type=MESH,
        )

    def arrive2(chunk, step):
        return pltpu.make_async_remote_copy(
            src_ref=out2.at[chunk, x],
            dst_ref=got2.at[chunk, x_peer(step)],
            send_sem=send2.at[chunk, step],
            recv_sem=recv2.at[chunk, x_peer(step)],
            device_id={"replica": x_peer(step) * 2 + z_lo},
            device_id_type=MESH,
        )

    def copy3(chunk, target):
        return pltpu.make_async_remote_copy(
            src_ref=out3.at[chunk],
            dst_ref=got3.at[chunk, z],
            send_sem=send3.at[chunk, target],
            recv_sem=recv3.at[chunk, z],
            device_id={"tensor": target, "replica": x * 2 + core},
            device_id_type=MESH,
        )

    def arrive3(chunk, far):
        return pltpu.make_async_remote_copy(
            src_ref=out3.at[chunk],
            dst_ref=got3.at[chunk, far],
            send_sem=send3.at[chunk, far],
            recv_sem=recv3.at[chunk, far],
            device_id={"tensor": (far // 2) * 2 + z_lo, "replica": x * 2 + far % 2},
            device_id_type=MESH,
        )

    def not_self(target):
        return jnp.logical_or(target != tensor, jnp.logical_not(same))

    def stage1(chunk):
        copy1(chunk).start()

    def stage2(chunk):
        copy1(chunk).wait_recv()
        total = acc[chunk, :, core] + got1[chunk]
        out2[chunk] = total
        for step in range(1, 8):
            copy2(chunk, step).start()

    def stage3(chunk):
        total = out2[chunk, x]
        for step in range(1, 8):
            arrive2(chunk, step).wait_recv()
            total = total + got2[chunk, x_peer(step)]
        out3[chunk] = total
        for target in range(8):

            @pl.when(not_self(target))
            def _():
                copy3(chunk, target).start()

        @pl.when(same)
        def _():
            got3[chunk, z] = out3[chunk]

    def finish(chunk):
        for far in range(8):

            @pl.when(jnp.logical_or(far != z, jnp.logical_not(same)))
            def _():
                arrive3(chunk, far).wait_recv()

        total = jnp.zeros((16, WIDTH), jnp.float32)
        for far in range(8):
            total = total + got3[chunk, far]
        sketch[chunk] = (total * (1.0 / 16)).astype(jnp.bfloat16)

    def back(chunk, first):
        for piece in range(PIECES):
            part = slice(piece * PIECE, (piece + 1) * PIECE)
            term = lax.dot_general(
                sketch[chunk],
                proj[chunk, part, :],
                (((1,), (1,)), ((), ())),
                preferred_element_type=jnp.float32,
            )
            out_ref[:, part] = term if first else out_ref[:, part] + term

    generate(0, 0, BLOCKS)
    for piece in range(PIECES):
        grad_copy(piece).wait()
    multiply(0)
    pl.semaphore_wait(barrier, jnp.where(same, 15, 16))
    stage1(0)
    generate(1, 0, 4)
    stage2(0)
    generate(1, 4, BLOCKS)
    multiply(1)
    stage1(1)
    stage3(0)
    stage2(1)
    finish(0)
    stage3(1)
    back(0, True)
    finish(1)
    back(1, False)
    for chunk in range(CHUNKS):
        copy1(chunk).wait_send()
        for step in range(1, 8):
            copy2(chunk, step).wait_send()
        for target in range(8):

            @pl.when(not_self(target))
            def _():
                copy3(chunk, target).wait_send()


def per_device(gradients, seeds, adam_step, first_moment, second_moment):
    gradient = pltpu.with_memory_space_constraint(gradients[0], pltpu.HBM)
    seeds = pltpu.with_memory_space_constraint(seeds, pltpu.HBM)
    dma = pltpu.SemaphoreType.DMA
    estimate = pl.pallas_call(
        kernel,
        out_shape=pltpu.VMEM((16, COLUMNS), jnp.float32),
        in_specs=[
            pl.BlockSpec(memory_space=pltpu.HBM),
            pl.BlockSpec(memory_space=pltpu.SMEM),
        ],
        out_specs=pl.BlockSpec(memory_space=pltpu.VMEM),
        scratch_shapes=[
            pltpu.VMEM((PIECES, 256, PIECE), jnp.bfloat16),
            pltpu.VMEM((CHUNKS, COLUMNS, WIDTH), jnp.bfloat16),
            pltpu.VMEM((DEPTH, WIDTH), jnp.int32),
            pltpu.VMEM((CHUNKS, 8, 2, 16, WIDTH), jnp.float32),
            pltpu.VMEM((CHUNKS, 8, 16, WIDTH), jnp.float32),
            pltpu.VMEM((CHUNKS, 8, 16, WIDTH), jnp.float32),
            pltpu.VMEM((CHUNKS, 8, 16, WIDTH), jnp.float32),
            pltpu.VMEM((CHUNKS, 16, WIDTH), jnp.float32),
            pltpu.VMEM((CHUNKS, 8, 16, WIDTH), jnp.float32),
            pltpu.VMEM((CHUNKS, 16, WIDTH), jnp.bfloat16),
            dma((PIECES,)),
            dma((CHUNKS,)),
            dma((CHUNKS,)),
            dma((CHUNKS, 8)),
            dma((CHUNKS, 8)),
            dma((CHUNKS, 8)),
            dma((CHUNKS, 8)),
        ],
        compiler_params=pltpu.CompilerParams(
            collective_id=0, has_side_effects=True, vmem_limit_bytes=24 << 20
        ),
        cost_estimate=pl.CostEstimate(
            flops=2 * 256 * COLUMNS * RANK, bytes_accessed=3 << 20, transcendentals=0
        ),
    )(gradient, seeds)
    new_first = 0.9 * first_moment + 0.1 * estimate
    new_second = 0.95 * second_moment + 0.05 * estimate * estimate
    step_float = adam_step[0].astype(jnp.float32)
    fix_first = 1.0 - jnp.power(jnp.float32(0.9), step_float)
    fix_second = 1.0 - jnp.power(jnp.float32(0.95), step_float)
    step_update = new_first / fix_first / (jnp.sqrt(new_second / fix_second) + 1e-08)
    return (new_first, new_second, step_update)


def solution(mesh):
    rows = P(("fsdp", "replica"), "tensor")
    return jax.shard_map(
        per_device,
        mesh=mesh,
        in_specs=(P("replica", "fsdp", "tensor"), P(), P(), rows, rows),
        out_specs=(rows, rows, rows),
        check_vma=False,
    )
```

```python
import math

import jax
import jax.numpy as jnp
from jax import lax
from jax.experimental import pallas as pl
from jax.experimental.pallas import tpu as pltpu
from jax.sharding import PartitionSpec as P

RANK = 512
COLUMNS = 3584
WIDTHS = (384, 128)
STARTS = (0, 384)
CHUNKS = len(WIDTHS)
DEPTH = 512
BLOCKS = COLUMNS // DEPTH
PIECE = 896
PIECES = COLUMNS // PIECE
X_ORDER = (4, 3, 5, 2, 6, 1, 7)
Z_ORDER = ((2, 0), (2, 1), (1, 0), (1, 1), (3, 0), (3, 1), (0, 1), (0, 0))
WEYL = -1640531535
MESH = pl.DeviceIdType.MESH
SINE = (6.28317941 / 16, -41.33894249 / 16, 81.39535834 / 16, -71.47469135 / 16)


def srl(value, bits):
    return lax.shift_right_logical(value, jnp.full_like(value, bits))


def scramble(value):
    value = value ^ srl(value, 16)
    value = value * jnp.int32(-2048144789)
    value = value ^ srl(value, 13)
    value = value * jnp.int32(-1028477387)
    return value ^ srl(value, 16)


def entries(counted, seed_key):
    hash_a = scramble(counted ^ seed_key)
    hash_b = scramble((counted + jnp.int32(WEYL)) ^ seed_key)
    negative_log = 16.635532333438686 - jnp.log(srl(hash_a, 8).astype(jnp.float32) + 0.5)
    radius = negative_log * lax.rsqrt(jnp.maximum(negative_log, 1e-30))
    turn = lax.shift_right_arithmetic(hash_b, jnp.full_like(hash_b, 8)).astype(jnp.float32) + 0.5
    z = 0.25 - jnp.abs(turn) * (1.0 / 16777216.0)
    square = z * z
    poly = SINE[3] * square + SINE[2]
    poly = poly * square + SINE[1]
    poly = poly * square + SINE[0]
    return (poly * z) * radius


def kernel(gradient_ref, seeds_ref, step_ref, out_ref, fix_ref, *scratch):
    grad, base, seeds, when = scratch[:4]
    per_chunk = [scratch[4 + i * CHUNKS : 4 + (i + 1) * CHUNKS] for i in range(7)]
    proj, acc, got1, out2, got2, out3, got3 = per_chunk
    sketch = scratch[4 + 7 * CHUNKS : 4 + 8 * CHUNKS]
    grad_sem, small_sem, send1, recv1, send2, recv2, send3, recv3 = scratch[4 + 8 * CHUNKS :]
    tensor = lax.axis_index("tensor")
    replica = lax.axis_index("replica")
    core = lax.rem(tensor, 2)
    z_hi = lax.div(tensor, 2)
    x = lax.div(replica, 2)
    z_lo = lax.rem(replica, 2)
    same = core == z_lo
    z = z_hi * 2 + z_lo

    def x_peer(step):
        return lax.rem(x + step, 8)

    seeds_copy = pltpu.make_async_copy(seeds_ref, seeds, small_sem.at[0])
    seeds_copy.start()

    barrier = pltpu.get_barrier_semaphore()
    pl.semaphore_signal(
        barrier, inc=1, device_id={"tensor": z_hi * 2 + 1 - core}, device_id_type=MESH
    )
    for step in range(1, 8):
        pl.semaphore_signal(
            barrier, inc=1, device_id={"replica": x_peer(step) * 2 + z_lo}, device_id_type=MESH
        )
    for far in range(8):
        far_hi, far_lo = far // 2, far % 2

        @pl.when(jnp.logical_or(far != z, jnp.logical_not(same)))
        def _():
            pl.semaphore_signal(
                barrier,
                inc=1,
                device_id={"tensor": far_hi * 2 + z_lo, "replica": x * 2 + far_lo},
                device_id_type=MESH,
            )

    def grad_copy(piece):
        return pltpu.make_async_copy(
            gradient_ref.at[:, pl.ds(piece * PIECE, PIECE)], grad.at[piece], grad_sem.at[piece]
        )

    for piece in range(PIECES):
        grad_copy(piece).start()

    rows = lax.broadcasted_iota(jnp.int32, base.shape, 0)
    lanes = lax.broadcasted_iota(jnp.int32, base.shape, 1)
    base[...] = (rows * jnp.int32(RANK) + lanes) * jnp.int32(2) * jnp.int32(WEYL)
    seeds_copy.wait()
    seed_key = seeds[0] ^ (seeds[1] * jnp.int32(668265263))
    first_column = tensor * COLUMNS

    def generate(chunk, lower, upper):
        def step(block, carry):
            start = pl.multiple_of(block * DEPTH, DEPTH)
            column = first_column + start
            offset = (column * jnp.int32(RANK) + STARTS[chunk]) * jnp.int32(2) * jnp.int32(WEYL)
            made = entries(base[:, : WIDTHS[chunk]] + offset, seed_key).astype(jnp.bfloat16)
            proj[chunk][pl.ds(start, DEPTH), :] = made
            return carry

        lax.fori_loop(lower, upper, step, 0)

    def multiply(chunk):
        part = None
        for piece in range(PIECES):
            term = jnp.dot(
                grad[piece],
                proj[chunk][piece * PIECE : (piece + 1) * PIECE, :],
                preferred_element_type=jnp.float32,
            )
            part = term if part is None else part + term
        acc[chunk][...] = part.reshape(8, 2, 16, WIDTHS[chunk])

    def copy1(chunk):
        return pltpu.make_async_remote_copy(
            src_ref=acc[chunk].at[:, 1 - core],
            dst_ref=got1[chunk],
            send_sem=send1.at[chunk],
            recv_sem=recv1.at[chunk],
            device_id={"tensor": z_hi * 2 + 1 - core},
            device_id_type=MESH,
        )

    def copy2(chunk, step):
        return pltpu.make_async_remote_copy(
            src_ref=out2[chunk].at[x_peer(step)],
            dst_ref=got2[chunk].at[x],
            send_sem=send2.at[chunk, step],
            recv_sem=recv2.at[chunk, x],
            device_id={"replica": x_peer(step) * 2 + z_lo},
            device_id_type=MESH,
        )

    def arrive2(chunk, step):
        return pltpu.make_async_remote_copy(
            src_ref=out2[chunk].at[x],
            dst_ref=got2[chunk].at[x_peer(step)],
            send_sem=send2.at[chunk, step],
            recv_sem=recv2.at[chunk, x_peer(step)],
            device_id={"replica": x_peer(step) * 2 + z_lo},
            device_id_type=MESH,
        )

    def copy3(chunk, number):
        ahead, other = Z_ORDER[number]
        target_core = 1 - core if other else core
        return pltpu.make_async_remote_copy(
            src_ref=out3[chunk],
            dst_ref=got3[chunk].at[z],
            send_sem=send3.at[chunk, number],
            recv_sem=recv3.at[chunk, z],
            device_id={
                "tensor": lax.rem(z_hi + ahead, 4) * 2 + target_core,
                "replica": x * 2 + core,
            },
            device_id_type=MESH,
        )

    def arrive3(chunk, far):
        return pltpu.make_async_remote_copy(
            src_ref=out3[chunk],
            dst_ref=got3[chunk].at[far],
            send_sem=send3.at[chunk, far],
            recv_sem=recv3.at[chunk, far],
            device_id={"tensor": (far // 2) * 2 + z_lo, "replica": x * 2 + far % 2},
            device_id_type=MESH,
        )

    def stage1(chunk):
        copy1(chunk).start()

    def stage2(chunk):
        copy1(chunk).wait_recv()
        out2[chunk][...] = acc[chunk][:, core] + got1[chunk][...]
        for step in X_ORDER:
            copy2(chunk, step).start()

    def stage3(chunk):
        total = out2[chunk][x]
        for step in range(1, 8):
            arrive2(chunk, step).wait_recv()
            total = total + got2[chunk][x_peer(step)]
        out3[chunk][...] = total
        for number in range(7):
            copy3(chunk, number).start()

        @pl.when(jnp.logical_not(same))
        def _():
            copy3(chunk, 7).start()

        @pl.when(same)
        def _():
            got3[chunk][z] = out3[chunk][...]

    def finish(chunk):
        for far in range(8):

            @pl.when(jnp.logical_or(far != z, jnp.logical_not(same)))
            def _():
                arrive3(chunk, far).wait_recv()

        total = got3[chunk][0]
        for far in range(1, 8):
            total = total + got3[chunk][far]
        sketch[chunk][...] = (total * (1.0 / 16)).astype(jnp.bfloat16)

    def back(chunk, first):
        for piece in range(PIECES):
            part = slice(piece * PIECE, (piece + 1) * PIECE)
            term = lax.dot_general(
                sketch[chunk][...],
                proj[chunk][part, :],
                (((1,), (1,)), ((), ())),
                preferred_element_type=jnp.float32,
            )
            out_ref[:, part] = term if first else out_ref[:, part] + term

    generate(0, 0, BLOCKS)
    for piece in range(PIECES):
        grad_copy(piece).wait()
    multiply(0)
    pl.semaphore_wait(barrier, jnp.where(same, 15, 16))
    stage1(0)
    generate(1, 0, 4)
    stage2(0)
    generate(1, 4, BLOCKS)
    multiply(1)
    stage1(1)
    stage2(1)
    stage3(0)
    steps = jnp.broadcast_to(step_ref[...], (8, 128)).astype(jnp.float32)
    first = lax.broadcasted_iota(jnp.int32, (8, 128), 0) < 4
    power = jnp.exp(steps * jnp.where(first, math.log(0.9), math.log(0.95)))
    fix_ref[...] = jnp.tile(1.0 / (1.0 - power), (1, COLUMNS // 128))
    stage3(1)
    finish(0)
    back(0, True)
    finish(1)
    back(1, False)
    for chunk in range(CHUNKS):
        copy1(chunk).wait_send()
        for step in X_ORDER:
            copy2(chunk, step).wait_send()
        for number in range(7):
            copy3(chunk, number).wait_send()

        @pl.when(jnp.logical_not(same))
        def _():
            copy3(chunk, 7).wait_send()


def per_device(gradients, seeds, adam_step, first_moment, second_moment):
    gradient = pltpu.with_memory_space_constraint(gradients[0], pltpu.HBM)
    seeds = pltpu.with_memory_space_constraint(seeds, pltpu.HBM)
    dma = pltpu.SemaphoreType.DMA
    estimate, fix = pl.pallas_call(
        kernel,
        out_shape=(pltpu.VMEM((16, COLUMNS), jnp.float32), pltpu.VMEM((8, COLUMNS), jnp.float32)),
        in_specs=[
            pl.BlockSpec(memory_space=pltpu.HBM),
            pl.BlockSpec(memory_space=pltpu.HBM),
            pl.BlockSpec(memory_space=pltpu.VMEM),
        ],
        out_specs=(pl.BlockSpec(memory_space=pltpu.VMEM), pl.BlockSpec(memory_space=pltpu.VMEM)),
        scratch_shapes=[
            pltpu.VMEM((PIECES, 256, PIECE), jnp.bfloat16),
            pltpu.VMEM((DEPTH, max(WIDTHS)), jnp.int32),
            pltpu.SMEM((2,), jnp.int32),
            pltpu.SMEM((1,), jnp.int32),
            *[pltpu.VMEM((COLUMNS, w), jnp.bfloat16) for w in WIDTHS],
            *[pltpu.VMEM((8, 2, 16, w), jnp.float32) for w in WIDTHS],
            *[pltpu.VMEM((8, 16, w), jnp.float32) for w in WIDTHS],
            *[pltpu.VMEM((8, 16, w), jnp.float32) for w in WIDTHS],
            *[pltpu.VMEM((8, 16, w), jnp.float32) for w in WIDTHS],
            *[pltpu.VMEM((16, w), jnp.float32) for w in WIDTHS],
            *[pltpu.VMEM((8, 16, w), jnp.float32) for w in WIDTHS],
            *[pltpu.VMEM((16, w), jnp.bfloat16) for w in WIDTHS],
            dma((PIECES,)),
            dma((2,)),
            dma((CHUNKS,)),
            dma((CHUNKS,)),
            dma((CHUNKS, 8)),
            dma((CHUNKS, 8)),
            dma((CHUNKS, 8)),
            dma((CHUNKS, 8)),
        ],
        compiler_params=pltpu.CompilerParams(
            collective_id=0, has_side_effects=True, vmem_limit_bytes=24 << 20
        ),
        cost_estimate=pl.CostEstimate(
            flops=2 * 256 * COLUMNS * RANK, bytes_accessed=3 << 20, transcendentals=0
        ),
    )(gradient, seeds, adam_step.reshape(1, 1))
    new_first = 0.9 * first_moment + 0.1 * estimate
    new_second = 0.95 * second_moment + 0.05 * estimate * estimate
    corrected = jnp.sqrt(new_second * fix[4:5]) + 1e-08
    step_update = new_first * fix[0:1] / corrected
    return (new_first, new_second, step_update)


def solution(mesh):
    rows = P(("fsdp", "replica"), "tensor")
    return jax.shard_map(
        per_device,
        mesh=mesh,
        in_specs=(P("replica", "fsdp", "tensor"), P(), P(), rows, rows),
        out_specs=(rows, rows, rows),
        check_vma=False,
    )
```

```python
import math

import jax
import jax.numpy as jnp
from jax import lax
from jax.experimental import pallas as pl
from jax.experimental.pallas import tpu as pltpu
from jax.sharding import PartitionSpec as P

RANK = 512
COLUMNS = 3584
WIDTHS = (384, 128)
STARTS = (0, 384)
WIRE = (jnp.float32, jnp.bfloat16)
CHUNKS = len(WIDTHS)
DEPTH = 512
BLOCKS = COLUMNS // DEPTH
X_ORDER = (4, 3, 5, 2, 6, 1, 7)
Z_ORDER = ((2, 0), (2, 1), (1, 0), (1, 1), (3, 0), (3, 1), (0, 1), (0, 0))
WEYL = -1640531535
MESH = pl.DeviceIdType.MESH
SINE = (6.28317941 / 16, -41.33894249 / 16, 81.39535834 / 16, -71.47469135 / 16)


def srl(value, bits):
    return lax.shift_right_logical(value, jnp.full_like(value, bits))


def scramble(value):
    value = value ^ srl(value, 16)
    value = value * jnp.int32(-2048144789)
    value = value ^ srl(value, 13)
    value = value * jnp.int32(-1028477387)
    return value ^ srl(value, 16)


def entries(counted, seed_key):
    hash_a = scramble(counted ^ seed_key)
    hash_b = scramble((counted + jnp.int32(WEYL)) ^ seed_key)
    negative_log = 16.635532333438686 - jnp.log(srl(hash_a, 8).astype(jnp.float32) + 0.5)
    radius = negative_log * lax.rsqrt(jnp.maximum(negative_log, 1e-30))
    turn = lax.shift_right_arithmetic(hash_b, jnp.full_like(hash_b, 8)).astype(jnp.float32) + 0.5
    z = 0.25 - jnp.abs(turn) * (1.0 / 16777216.0)
    square = z * z
    poly = SINE[3] * square + SINE[2]
    poly = poly * square + SINE[1]
    poly = poly * square + SINE[0]
    return (poly * z) * radius


def kernel(gradient_ref, seeds_ref, step_ref, out_ref, fix_ref, *scratch):
    grad, base, seeds = scratch[:3]
    per_chunk = [scratch[3 + i * CHUNKS : 3 + (i + 1) * CHUNKS] for i in range(7)]
    proj, acc, got1, out2, got2, out3, got3 = per_chunk
    sketch = scratch[3 + 7 * CHUNKS : 3 + 8 * CHUNKS]
    small_sem, send1, recv1, send2, recv2, send3, recv3 = scratch[3 + 8 * CHUNKS :]
    tensor = lax.axis_index("tensor")
    replica = lax.axis_index("replica")
    core = lax.rem(tensor, 2)
    z_hi = lax.div(tensor, 2)
    x = lax.div(replica, 2)
    z_lo = lax.rem(replica, 2)
    same = core == z_lo
    z = z_hi * 2 + z_lo

    def x_peer(step):
        return lax.rem(x + step, 8)

    seeds_copy = pltpu.make_async_copy(seeds_ref, seeds, small_sem.at[0])
    seeds_copy.start()

    barrier = pltpu.get_barrier_semaphore()
    pl.semaphore_signal(
        barrier, inc=1, device_id={"tensor": z_hi * 2 + 1 - core}, device_id_type=MESH
    )
    for step in range(1, 8):
        pl.semaphore_signal(
            barrier, inc=1, device_id={"replica": x_peer(step) * 2 + z_lo}, device_id_type=MESH
        )
    for far in range(8):
        far_hi, far_lo = far // 2, far % 2

        @pl.when(jnp.logical_or(far != z, jnp.logical_not(same)))
        def _():
            pl.semaphore_signal(
                barrier,
                inc=1,
                device_id={"tensor": far_hi * 2 + z_lo, "replica": x * 2 + far_lo},
                device_id_type=MESH,
            )

    grad_copy = pltpu.make_async_copy(gradient_ref, grad, small_sem.at[1])
    grad_copy.start()

    rows = lax.broadcasted_iota(jnp.int32, base.shape, 0)
    lanes = lax.broadcasted_iota(jnp.int32, base.shape, 1)
    base[...] = (rows * jnp.int32(RANK) + lanes) * jnp.int32(2) * jnp.int32(WEYL)
    seeds_copy.wait()
    seed_key = seeds[0] ^ (seeds[1] * jnp.int32(668265263))
    first_column = tensor * COLUMNS

    def generate(chunk, lower, upper):
        def step(block, carry):
            start = pl.multiple_of(block * DEPTH, DEPTH)
            column = first_column + start
            offset = (column * jnp.int32(RANK) + STARTS[chunk]) * jnp.int32(2) * jnp.int32(WEYL)
            made = entries(base[:, : WIDTHS[chunk]] + offset, seed_key).astype(jnp.bfloat16)
            proj[chunk][pl.ds(start, DEPTH), :] = made
            return carry

        lax.fori_loop(lower, upper, step, 0)

    def multiply(chunk):
        part = jnp.dot(grad[...], proj[chunk][...], preferred_element_type=jnp.float32)
        acc[chunk][...] = part.reshape(8, 2, 16, WIDTHS[chunk])

    def copy1(chunk):
        return pltpu.make_async_remote_copy(
            src_ref=acc[chunk].at[:, 1 - core],
            dst_ref=got1[chunk],
            send_sem=send1.at[chunk],
            recv_sem=recv1.at[chunk],
            device_id={"tensor": z_hi * 2 + 1 - core},
            device_id_type=MESH,
        )

    def copy2(chunk, step):
        return pltpu.make_async_remote_copy(
            src_ref=out2[chunk].at[x_peer(step)],
            dst_ref=got2[chunk].at[x],
            send_sem=send2.at[chunk, step],
            recv_sem=recv2.at[chunk, x],
            device_id={"replica": x_peer(step) * 2 + z_lo},
            device_id_type=MESH,
        )

    def arrive2(chunk, step):
        return pltpu.make_async_remote_copy(
            src_ref=out2[chunk].at[x],
            dst_ref=got2[chunk].at[x_peer(step)],
            send_sem=send2.at[chunk, step],
            recv_sem=recv2.at[chunk, x_peer(step)],
            device_id={"replica": x_peer(step) * 2 + z_lo},
            device_id_type=MESH,
        )

    def copy3(chunk, number):
        ahead, other = Z_ORDER[number]
        target_core = 1 - core if other else core
        return pltpu.make_async_remote_copy(
            src_ref=out3[chunk],
            dst_ref=got3[chunk].at[z],
            send_sem=send3.at[chunk, number],
            recv_sem=recv3.at[chunk, z],
            device_id={
                "tensor": lax.rem(z_hi + ahead, 4) * 2 + target_core,
                "replica": x * 2 + core,
            },
            device_id_type=MESH,
        )

    def arrive3(chunk, far):
        return pltpu.make_async_remote_copy(
            src_ref=out3[chunk],
            dst_ref=got3[chunk].at[far],
            send_sem=send3.at[chunk, far],
            recv_sem=recv3.at[chunk, far],
            device_id={"tensor": (far // 2) * 2 + z_lo, "replica": x * 2 + far % 2},
            device_id_type=MESH,
        )

    def stage1(chunk):
        copy1(chunk).start()

    def stage2(chunk):
        copy1(chunk).wait_recv()
        out2[chunk][...] = (acc[chunk][:, core] + got1[chunk][...]).astype(WIRE[chunk])
        for step in X_ORDER:
            copy2(chunk, step).start()

    def stage3(chunk):
        total = acc[chunk][x, core] + got1[chunk][x]
        for step in range(1, 8):
            arrive2(chunk, step).wait_recv()
            total = total + got2[chunk][x_peer(step)].astype(jnp.float32)
        out3[chunk][...] = total.astype(WIRE[chunk])
        for number in range(7):
            copy3(chunk, number).start()

        @pl.when(jnp.logical_not(same))
        def _():
            copy3(chunk, 7).start()

        @pl.when(same)
        def _():
            got3[chunk][z] = out3[chunk][...]

    def finish(chunk):
        for far in range(8):

            @pl.when(jnp.logical_or(far != z, jnp.logical_not(same)))
            def _():
                arrive3(chunk, far).wait_recv()

        total = got3[chunk][0].astype(jnp.float32)
        for far in range(1, 8):
            total = total + got3[chunk][far].astype(jnp.float32)
        sketch[chunk][...] = (total * (1.0 / 16)).astype(jnp.bfloat16)

    def back(chunk, first):
        for start in range(0, COLUMNS, DEPTH):
            part = slice(start, start + DEPTH)
            term = lax.dot_general(
                sketch[chunk][...],
                proj[chunk][part, :],
                (((1,), (1,)), ((), ())),
                preferred_element_type=jnp.float32,
            )
            out_ref[:, part] = term if first else out_ref[:, part] + term

    generate(0, 0, BLOCKS)
    grad_copy.wait()
    multiply(0)
    pl.semaphore_wait(barrier, jnp.where(same, 15, 16))
    stage1(0)
    generate(1, 0, 4)
    stage2(0)
    generate(1, 4, BLOCKS)
    multiply(1)
    stage1(1)
    stage2(1)
    stage3(0)
    steps = jnp.broadcast_to(step_ref[...], (8, 128)).astype(jnp.float32)
    first = lax.broadcasted_iota(jnp.int32, (8, 128), 0) < 4
    power = jnp.exp(steps * jnp.where(first, math.log(0.9), math.log(0.95)))
    fix_ref[...] = jnp.tile(1.0 / (1.0 - power), (1, COLUMNS // 128))
    stage3(1)
    finish(0)
    back(0, True)
    finish(1)
    back(1, False)
    for chunk in range(CHUNKS):
        copy1(chunk).wait_send()
        for step in X_ORDER:
            copy2(chunk, step).wait_send()
        for number in range(7):
            copy3(chunk, number).wait_send()

        @pl.when(jnp.logical_not(same))
        def _():
            copy3(chunk, 7).wait_send()


def per_device(gradients, seeds, adam_step, first_moment, second_moment):
    gradient = pltpu.with_memory_space_constraint(gradients[0], pltpu.HBM)
    seeds = pltpu.with_memory_space_constraint(seeds, pltpu.HBM)
    dma = pltpu.SemaphoreType.DMA
    estimate, fix = pl.pallas_call(
        kernel,
        out_shape=(pltpu.VMEM((16, COLUMNS), jnp.float32), pltpu.VMEM((8, COLUMNS), jnp.float32)),
        in_specs=[
            pl.BlockSpec(memory_space=pltpu.HBM),
            pl.BlockSpec(memory_space=pltpu.HBM),
            pl.BlockSpec(memory_space=pltpu.VMEM),
        ],
        out_specs=(pl.BlockSpec(memory_space=pltpu.VMEM), pl.BlockSpec(memory_space=pltpu.VMEM)),
        scratch_shapes=[
            pltpu.VMEM((256, COLUMNS), jnp.bfloat16),
            pltpu.VMEM((DEPTH, max(WIDTHS)), jnp.int32),
            pltpu.SMEM((2,), jnp.int32),
            *[pltpu.VMEM((COLUMNS, w), jnp.bfloat16) for w in WIDTHS],
            *[pltpu.VMEM((8, 2, 16, w), jnp.float32) for w in WIDTHS],
            *[pltpu.VMEM((8, 16, w), jnp.float32) for w in WIDTHS],
            *[pltpu.VMEM((8, 16, w), t) for w, t in zip(WIDTHS, WIRE)],
            *[pltpu.VMEM((8, 16, w), t) for w, t in zip(WIDTHS, WIRE)],
            *[pltpu.VMEM((16, w), t) for w, t in zip(WIDTHS, WIRE)],
            *[pltpu.VMEM((8, 16, w), t) for w, t in zip(WIDTHS, WIRE)],
            *[pltpu.VMEM((16, w), jnp.bfloat16) for w in WIDTHS],
            dma((2,)),
            dma((CHUNKS,)),
            dma((CHUNKS,)),
            dma((CHUNKS, 8)),
            dma((CHUNKS, 8)),
            dma((CHUNKS, 8)),
            dma((CHUNKS, 8)),
        ],
        compiler_params=pltpu.CompilerParams(
            collective_id=0, has_side_effects=True, vmem_limit_bytes=24 << 20
        ),
        cost_estimate=pl.CostEstimate(
            flops=2 * 256 * COLUMNS * RANK, bytes_accessed=3 << 20, transcendentals=0
        ),
    )(gradient, seeds, adam_step.reshape(1, 1))
    new_first = 0.9 * first_moment + 0.1 * estimate
    new_second = 0.95 * second_moment + 0.05 * estimate * estimate
    corrected = jnp.sqrt(new_second * fix[4:5]) + 1e-08
    step_update = new_first * fix[0:1] / corrected
    return (new_first, new_second, step_update)


def solution(mesh):
    rows = P(("fsdp", "replica"), "tensor")
    return jax.shard_map(
        per_device,
        mesh=mesh,
        in_specs=(P("replica", "fsdp", "tensor"), P(), P(), rows, rows),
        out_specs=(rows, rows, rows),
        check_vma=False,
    )
```

```python
import math

import jax
import jax.numpy as jnp
from jax import lax
from jax.experimental import pallas as pl
from jax.experimental.pallas import tpu as pltpu
from jax.sharding import PartitionSpec as P

RANK = 512
COLUMNS = 3584
WIDTHS = (384, 128)
STARTS = (0, 384)
WIRE = (jnp.float32, jnp.bfloat16)
CHUNKS = len(WIDTHS)
DEPTH = 896
BLOCKS = COLUMNS // DEPTH
X_ORDER = (4, 3, 5, 2, 6, 1, 7)
Z_ORDER = ((2, 0), (2, 1), (1, 0), (1, 1), (3, 0), (3, 1), (0, 1), (0, 0))
WEYL = -1640531535
MESH = pl.DeviceIdType.MESH
SINE = (6.28317941 / 16, -41.33894249 / 16, 81.39535834 / 16, -71.47469135 / 16)
SCALE = -((-SINE[3]) ** (1.0 / 7.0))
MONIC = tuple(SINE[k] / SCALE ** (2 * k + 1) for k in range(3))


def srl(value, bits):
    return lax.shift_right_logical(value, jnp.full_like(value, bits))


def scramble(value):
    value = value ^ srl(value, 16)
    value = value * jnp.int32(-2048144789)
    value = value ^ srl(value, 13)
    value = value * jnp.int32(-1028477387)
    return value ^ srl(value, 16)


def entries(counted, seed_key):
    hash_a = scramble(counted ^ seed_key)
    hash_b = scramble((counted + jnp.int32(WEYL)) ^ seed_key)
    negative_log = 16.635532333438686 - jnp.log(srl(hash_a, 8).astype(jnp.float32) + 0.5)
    radius = negative_log * lax.rsqrt(jnp.maximum(negative_log, 1e-30))
    turn = lax.shift_right_arithmetic(hash_b, jnp.full_like(hash_b, 8)).astype(jnp.float32) + 0.5
    y = SCALE / 4 - jnp.abs(turn) * (SCALE / 16777216.0)
    square = y * y
    poly = (square + MONIC[2]) * square + MONIC[1]
    poly = poly * square + MONIC[0]
    return (poly * y) * radius


def kernel(gradient_ref, seeds_ref, step_ref, out_ref, fix_ref, *scratch):
    grad, base, seeds = scratch[:3]
    per_chunk = [scratch[3 + i * CHUNKS : 3 + (i + 1) * CHUNKS] for i in range(7)]
    proj, acc, got1, out2, got2, out3, got3 = per_chunk
    sketch = scratch[3 + 7 * CHUNKS : 3 + 8 * CHUNKS]
    small_sem, send1, recv1, send2, recv2, send3, recv3 = scratch[3 + 8 * CHUNKS :]
    tensor = lax.axis_index("tensor")
    replica = lax.axis_index("replica")
    core = lax.rem(tensor, 2)
    z_hi = lax.div(tensor, 2)
    x = lax.div(replica, 2)
    z_lo = lax.rem(replica, 2)
    same = core == z_lo
    z = z_hi * 2 + z_lo

    def x_peer(step):
        return lax.rem(x + step, 8)

    seeds_copy = pltpu.make_async_copy(seeds_ref, seeds, small_sem.at[0])
    seeds_copy.start()

    barrier = pltpu.get_barrier_semaphore()
    pl.semaphore_signal(
        barrier, inc=1, device_id={"tensor": z_hi * 2 + 1 - core}, device_id_type=MESH
    )
    for step in range(1, 8):
        pl.semaphore_signal(
            barrier, inc=1, device_id={"replica": x_peer(step) * 2 + z_lo}, device_id_type=MESH
        )
    for far in range(8):
        far_hi, far_lo = far // 2, far % 2

        @pl.when(jnp.logical_or(far != z, jnp.logical_not(same)))
        def _():
            pl.semaphore_signal(
                barrier,
                inc=1,
                device_id={"tensor": far_hi * 2 + z_lo, "replica": x * 2 + far_lo},
                device_id_type=MESH,
            )

    grad_copy = pltpu.make_async_copy(gradient_ref, grad, small_sem.at[1])
    grad_copy.start()

    rows = lax.broadcasted_iota(jnp.int32, base.shape, 0)
    lanes = lax.broadcasted_iota(jnp.int32, base.shape, 1)
    base[...] = (rows * jnp.int32(RANK) + lanes) * jnp.int32(2) * jnp.int32(WEYL)
    seeds_copy.wait()
    seed_key = seeds[0] ^ (seeds[1] * jnp.int32(668265263))
    first_column = tensor * COLUMNS

    def generate(chunk, lower, upper):
        def step(block, carry):
            start = pl.multiple_of(block * DEPTH, DEPTH)
            column = first_column + start
            offset = (column * jnp.int32(RANK) + STARTS[chunk]) * jnp.int32(2) * jnp.int32(WEYL)
            made = entries(base[:, : WIDTHS[chunk]] + offset, seed_key).astype(jnp.bfloat16)
            proj[chunk][pl.ds(start, DEPTH), :] = made
            return carry

        lax.fori_loop(lower, upper, step, 0)

    def multiply(chunk):
        part = jnp.dot(grad[...], proj[chunk][...], preferred_element_type=jnp.float32)
        acc[chunk][...] = part.reshape(8, 2, 16, WIDTHS[chunk])

    def copy1(chunk):
        return pltpu.make_async_remote_copy(
            src_ref=acc[chunk].at[:, 1 - core],
            dst_ref=got1[chunk],
            send_sem=send1.at[chunk],
            recv_sem=recv1.at[chunk],
            device_id={"tensor": z_hi * 2 + 1 - core},
            device_id_type=MESH,
        )

    def copy2(chunk, step):
        return pltpu.make_async_remote_copy(
            src_ref=out2[chunk].at[x_peer(step)],
            dst_ref=got2[chunk].at[x],
            send_sem=send2.at[chunk, step],
            recv_sem=recv2.at[chunk, x],
            device_id={"replica": x_peer(step) * 2 + z_lo},
            device_id_type=MESH,
        )

    def arrive2(chunk, step):
        return pltpu.make_async_remote_copy(
            src_ref=out2[chunk].at[x],
            dst_ref=got2[chunk].at[x_peer(step)],
            send_sem=send2.at[chunk, step],
            recv_sem=recv2.at[chunk, x_peer(step)],
            device_id={"replica": x_peer(step) * 2 + z_lo},
            device_id_type=MESH,
        )

    def copy3(chunk, number):
        ahead, other = Z_ORDER[number]
        target_core = 1 - core if other else core
        return pltpu.make_async_remote_copy(
            src_ref=out3[chunk],
            dst_ref=got3[chunk].at[z],
            send_sem=send3.at[chunk, number],
            recv_sem=recv3.at[chunk, z],
            device_id={
                "tensor": lax.rem(z_hi + ahead, 4) * 2 + target_core,
                "replica": x * 2 + core,
            },
            device_id_type=MESH,
        )

    def arrive3(chunk, far):
        return pltpu.make_async_remote_copy(
            src_ref=out3[chunk],
            dst_ref=got3[chunk].at[far],
            send_sem=send3.at[chunk, far],
            recv_sem=recv3.at[chunk, far],
            device_id={"tensor": (far // 2) * 2 + z_lo, "replica": x * 2 + far % 2},
            device_id_type=MESH,
        )

    def stage1(chunk):
        copy1(chunk).start()

    def stage2(chunk):
        copy1(chunk).wait_recv()
        out2[chunk][...] = (acc[chunk][:, core] + got1[chunk][...]).astype(WIRE[chunk])
        for step in X_ORDER:
            copy2(chunk, step).start()

    def stage3(chunk):
        total = acc[chunk][x, core] + got1[chunk][x]
        for step in range(1, 8):
            arrive2(chunk, step).wait_recv()
            total = total + got2[chunk][x_peer(step)].astype(jnp.float32)
        out3[chunk][...] = total.astype(WIRE[chunk])
        for number in range(7):
            copy3(chunk, number).start()

        @pl.when(jnp.logical_not(same))
        def _():
            copy3(chunk, 7).start()

        @pl.when(same)
        def _():
            got3[chunk][z] = out3[chunk][...]

    def finish(chunk):
        for far in range(8):

            @pl.when(jnp.logical_or(far != z, jnp.logical_not(same)))
            def _():
                arrive3(chunk, far).wait_recv()

        total = got3[chunk][0].astype(jnp.float32)
        for far in range(1, 8):
            total = total + got3[chunk][far].astype(jnp.float32)
        sketch[chunk][...] = (total * (1.0 / 16)).astype(jnp.bfloat16)

    def back(chunk, first):
        for start in range(0, COLUMNS, DEPTH):
            part = slice(start, start + DEPTH)
            term = lax.dot_general(
                sketch[chunk][...],
                proj[chunk][part, :],
                (((1,), (1,)), ((), ())),
                preferred_element_type=jnp.float32,
            )
            out_ref[:, part] = term if first else out_ref[:, part] + term

    generate(0, 0, BLOCKS)
    grad_copy.wait()
    multiply(0)
    pl.semaphore_wait(barrier, jnp.where(same, 15, 16))
    stage1(0)
    generate(1, 0, 2)
    stage2(0)
    generate(1, 2, BLOCKS)
    multiply(1)
    stage1(1)
    stage2(1)
    stage3(0)
    steps = jnp.broadcast_to(step_ref[...], (8, 128)).astype(jnp.float32)
    first = lax.broadcasted_iota(jnp.int32, (8, 128), 0) < 4
    power = jnp.exp(steps * jnp.where(first, math.log(0.9), math.log(0.95)))
    fix_ref[...] = jnp.tile(1.0 / (1.0 - power), (1, COLUMNS // 128))
    stage3(1)
    finish(0)
    back(0, True)
    finish(1)
    back(1, False)
    for chunk in range(CHUNKS):
        copy1(chunk).wait_send()
        for step in X_ORDER:
            copy2(chunk, step).wait_send()
        for number in range(7):
            copy3(chunk, number).wait_send()

        @pl.when(jnp.logical_not(same))
        def _():
            copy3(chunk, 7).wait_send()


def per_device(gradients, seeds, adam_step, first_moment, second_moment):
    gradient = pltpu.with_memory_space_constraint(gradients[0], pltpu.HBM)
    seeds = pltpu.with_memory_space_constraint(seeds, pltpu.HBM)
    dma = pltpu.SemaphoreType.DMA
    estimate, fix = pl.pallas_call(
        kernel,
        out_shape=(pltpu.VMEM((16, COLUMNS), jnp.float32), pltpu.VMEM((8, COLUMNS), jnp.float32)),
        in_specs=[
            pl.BlockSpec(memory_space=pltpu.HBM),
            pl.BlockSpec(memory_space=pltpu.HBM),
            pl.BlockSpec(memory_space=pltpu.VMEM),
        ],
        out_specs=(pl.BlockSpec(memory_space=pltpu.VMEM), pl.BlockSpec(memory_space=pltpu.VMEM)),
        scratch_shapes=[
            pltpu.VMEM((256, COLUMNS), jnp.bfloat16),
            pltpu.VMEM((DEPTH, max(WIDTHS)), jnp.int32),
            pltpu.SMEM((2,), jnp.int32),
            *[pltpu.VMEM((COLUMNS, w), jnp.bfloat16) for w in WIDTHS],
            *[pltpu.VMEM((8, 2, 16, w), jnp.float32) for w in WIDTHS],
            *[pltpu.VMEM((8, 16, w), jnp.float32) for w in WIDTHS],
            *[pltpu.VMEM((8, 16, w), t) for w, t in zip(WIDTHS, WIRE)],
            *[pltpu.VMEM((8, 16, w), t) for w, t in zip(WIDTHS, WIRE)],
            *[pltpu.VMEM((16, w), t) for w, t in zip(WIDTHS, WIRE)],
            *[pltpu.VMEM((8, 16, w), t) for w, t in zip(WIDTHS, WIRE)],
            *[pltpu.VMEM((16, w), jnp.bfloat16) for w in WIDTHS],
            dma((2,)),
            dma((CHUNKS,)),
            dma((CHUNKS,)),
            dma((CHUNKS, 8)),
            dma((CHUNKS, 8)),
            dma((CHUNKS, 8)),
            dma((CHUNKS, 8)),
        ],
        compiler_params=pltpu.CompilerParams(
            collective_id=0, has_side_effects=True, vmem_limit_bytes=24 << 20
        ),
        cost_estimate=pl.CostEstimate(
            flops=2 * 256 * COLUMNS * RANK, bytes_accessed=3 << 20, transcendentals=0
        ),
    )(gradient, seeds, adam_step.reshape(1, 1))
    new_first = 0.9 * first_moment + 0.1 * estimate
    new_second = 0.95 * second_moment + 0.05 * estimate * estimate
    corrected = jnp.sqrt(new_second * fix[4:5]) + 1e-08
    step_update = new_first * fix[0:1] / corrected
    return (new_first, new_second, step_update)


def solution(mesh):
    rows = P(("fsdp", "replica"), "tensor")
    return jax.shard_map(
        per_device,
        mesh=mesh,
        in_specs=(P("replica", "fsdp", "tensor"), P(), P(), rows, rows),
        out_specs=(rows, rows, rows),
        check_vma=False,
    )
```
